128 devices in a mesh: dp: 4 (over z), expert: 32 (over y, x, core).
Axes of the slice: x: 4, y: 4, z: 4, core: 2. Of those that a mesh axis runs over, the one named last changes fastest.
Arguments:
- tokens: bfloat16 [16384, 4096], P(('dp', 'expert')), may hold values from -6 to 6
- expert_ids: int32 [16384, 2], P(('dp', 'expert')), may hold values from 0 to 31, all different within a row; in each aligned block of 128 rows (0 to 127, 128 to 255, ...) at most 9 rows name the same one
- router_probs: float32 [16384, 2], P(('dp', 'expert')), may hold values from 0.1 to 1
- w_gate: bfloat16 [32, 1024, 4096], P('expert', 'dp'), may hold values from -0.09375 to 0.09375
- w_up: bfloat16 [32, 1024, 4096], P('expert', 'dp'), may hold values from -0.09375 to 0.09375
- w_down: bfloat16 [32, 1024, 4096], P('expert', 'dp'), may hold values from -0.1875 to 0.1875
- out_grad: bfloat16 [16384, 4096], P(('dp', 'expert')), may hold values from -6 to 6
Outputs:
- mixed: bfloat16 [16384, 4096], P(('dp', 'expert'))
- input_grad: bfloat16 [16384, 4096], P(('dp', 'expert'))
- prob_grad: float32 [16384, 2], P(('dp', 'expert'))
- grad_gate: bfloat16 [32, 1024, 4096], P('expert', 'dp')
- grad_up: bfloat16 [32, 1024, 4096], P('expert', 'dp')
- grad_down: bfloat16 [32, 1024, 4096], P('expert', 'dp')
The draws below stay inside these ranges and needn't reach their ends.
Inputs may be any that keep to these rules, and one draw needn't show every extreme that they name: `expert_ids`: each row names 2 different experts. Among the rows of one device no expert is named more than 9 times, a bound that some block reaches.
All inputs are finite; a program needn't handle non-finite values.
Results may differ from the reference program's by a relative error of at most 0.018.
Values may be sent and summed in bfloat16 or wider, within the bound.
No kernel may reach another device: no remote copies, remote signals or barrier semaphores. Data moves between devices by JAX's collectives and lax.ppermute only.
A program may use at most 192 MiB of HBM per device.

```python
import math
import jax
import jax.numpy as jnp
import numpy as np
from jax import lax

D = 4096
FFW = 1024
TOPK = 2
TOK_DEV = 128
EXPERTS = 32
MOST = 9
TOKENS = 16384
N_DP = 4
N_EXPERT = 32


def steps_of(own_key, dims, split, low, top_value):
    level, own = 1.0, jax.random.fold_in(own_key, 6)
    for axis_at, shards_of in split:
        steps = jnp.exp(jax.random.uniform(jax.random.fold_in(own, axis_at), (shards_of,), jnp.float32, low / len(split), top_value / len(split)))
        level = level * jnp.repeat(steps, dims[axis_at] // shards_of).reshape([-1 if axis == axis_at else 1 for axis in range(len(dims))])
    return level


def assign_block(key, own, number, rows, count, top, most, skew):
    ranking = jax.random.permutation(key, count)
    packed, common = load_shares(count, rows * top, most, skew, True), load_shares(count, rows * top, most, skew, False)
    places = jnp.arange(count)

    def named(lengths, turn):
        used = int((lengths > 0).sum())
        fixed = max(1, used // 4)
        passed = fixed + (places - fixed + turn * (used - fixed)) % max(1, count - fixed)
        return jnp.zeros((count,), jnp.int32).at[ranking[jnp.where(places < fixed, places, passed)]].set(jnp.asarray(lengths, jnp.int32))

    lengths = jnp.where(number % 4 == 0, named(packed, number // 4), named(common, number - number // 4 - 1))
    mixed = jax.random.permutation(jax.random.fold_in(own, 3), count)
    donor, receiver = mixed[0:count // 2 * 2:2], mixed[1:count // 2 * 2:2]
    margin = jnp.minimum(lengths[donor] - 1, most - lengths[receiver]) // 2
    margin = jnp.where((donor == ranking[0]) | (receiver == ranking[0]) | (lengths[receiver] == 0), 0, jnp.maximum(margin, 0))
    passed = jax.random.randint(jax.random.fold_in(own, 4), (count // 2,), 0, 1 << 20) % (margin + 1)
    lengths = lengths.at[donor].add(-passed).at[receiver].add(passed)
    items = jnp.searchsorted(jnp.cumsum(lengths), jnp.arange(rows * top), side="right").astype(jnp.int32)
    listing = items.reshape(top, rows).T
    listing = listing[jax.random.permutation(jax.random.fold_in(own, 1), rows)]
    turn = jax.random.randint(jax.random.fold_in(own, 2), (rows, 1), 0, top)
    return jnp.take_along_axis(listing, (jnp.arange(top)[None, :] + turn) % top, axis=1)


def load_shares(count, total, limit, lean, full):
    loads = [(1 << 20) // math.isqrt(rank ** lean) + 1 for rank in range(1, count + 1)]
    largest = limit if full else min(limit, max(-(-total // count), total * loads[0] // sum(loads)))
    least = 1 if total - largest >= count - 1 else 0
    counts, spare = [largest] + [least] * (count - 1), total - largest - least * (count - 1)
    while spare > 0:
        movable = [i for i in range(1, count) if counts[i] < largest] or [i for i in range(1, count) if counts[i] < limit]
        mass, remaining = sum([loads[i] for i in movable]), spare
        for i in movable:
            extra = min(limit - counts[i], max(1, remaining * loads[i] // mass), spare)
            counts[i] = counts[i] + extra
            spare = spare - extra
    return np.array(counts)


def bell_draw(key, dims, width, limit, pieces=(), kind=jnp.bfloat16):
    drawn = width * jax.random.normal(key, dims, jnp.float32)
    if pieces:
        drawn = drawn * steps_of(key, dims, pieces, -0.22, 0.18)
    return jnp.clip(drawn, -limit, limit).astype(kind)


def setup_inputs(seed: int = 0) -> dict:
    splits = jax.random.split(jax.random.key(seed), 8)
    tokens = bell_draw(splits[0], (TOKENS, D), 1.0, 6.0, ((0, 128),))
    expert_ids_keys = jax.random.split(jax.random.fold_in(splits[1], 1), TOKENS // TOK_DEV)
    expert_ids_turns = jax.random.permutation(jax.random.fold_in(splits[1], 3), TOKENS // TOK_DEV)
    expert_ids = jax.vmap(lambda own, number: assign_block(jax.random.fold_in(splits[1], 2), own, number, TOK_DEV, EXPERTS, TOPK, MOST, 2))(expert_ids_keys, expert_ids_turns).reshape((TOKENS, TOPK))
    router_probs = jnp.clip(0.1 + 0.9 * jax.random.uniform(splits[2], (TOKENS, TOPK), jnp.float32) ** steps_of(splits[2], (TOKENS, TOPK), ((0, 128),), -0.2, 0.2), 0.1, 1.0)
    w_gate = bell_draw(splits[3], (EXPERTS, FFW, D), D ** -0.5, 0.09375, ((0, 32), (1, 4)))
    w_up = bell_draw(splits[4], (EXPERTS, FFW, D), D ** -0.5, 0.09375, ((0, 32), (1, 4)))
    w_down = bell_draw(splits[5], (EXPERTS, FFW, D), FFW ** -0.5, 0.1875, ((0, 32), (1, 4)))
    out_grad = bell_draw(splits[6], (TOKENS, D), 1.0, 6.0, ((0, 128),))
    return dict(tokens=tokens, expert_ids=expert_ids, router_probs=router_probs, w_gate=w_gate, w_up=w_up, w_down=w_down, out_grad=out_grad)


def expert_pass(tok_slots, grad_slots, gate_w, up_w, down_w):
    gate_proj = jnp.dot(tok_slots, gate_w.T, preferred_element_type=jnp.float32)
    up_proj = jnp.dot(tok_slots, up_w.T, preferred_element_type=jnp.float32)
    sigmoid_gate = jax.nn.sigmoid(gate_proj)
    activated = gate_proj * sigmoid_gate
    hidden = (activated * up_proj).astype(jnp.bfloat16)
    d_hidden = jnp.dot(grad_slots, down_w.T, preferred_element_type=jnp.float32)
    d_gate = (d_hidden * up_proj * sigmoid_gate * (1.0 + gate_proj * (1.0 - sigmoid_gate))).astype(jnp.bfloat16)
    d_up = (d_hidden * activated).astype(jnp.bfloat16)
    quarter_width = FFW // N_DP
    out_sum = jnp.zeros((tok_slots.shape[0], D), jnp.float32)
    back_sum = jnp.zeros((tok_slots.shape[0], D), jnp.float32)
    for part_index in range(N_DP):
        lower = part_index * quarter_width
        upper = lower + quarter_width
        part_out = jnp.dot(hidden[:, lower:upper], down_w[lower:upper], preferred_element_type=jnp.float32)
        part_out = lax.optimization_barrier(part_out.astype(jnp.bfloat16))
        out_sum = out_sum + part_out.astype(jnp.float32)
        part_back = jnp.dot(d_gate[:, lower:upper], gate_w[lower:upper], preferred_element_type=jnp.float32)
        part_back = part_back + jnp.dot(d_up[:, lower:upper], up_w[lower:upper], preferred_element_type=jnp.float32)
        part_back = lax.optimization_barrier(part_back.astype(jnp.bfloat16))
        back_sum = back_sum + part_back.astype(jnp.float32)
    grad_down_e = jnp.dot(hidden.T, grad_slots, preferred_element_type=jnp.float32).astype(jnp.bfloat16)
    grad_gate_e = jnp.dot(d_gate.T, tok_slots, preferred_element_type=jnp.float32).astype(jnp.bfloat16)
    grad_up_e = jnp.dot(d_up.T, tok_slots, preferred_element_type=jnp.float32).astype(jnp.bfloat16)
    return out_sum.astype(jnp.bfloat16), back_sum.astype(jnp.bfloat16), grad_gate_e, grad_up_e, grad_down_e


def reference(tokens, expert_ids, router_probs, w_gate, w_up, w_down, out_grad):
    devices = N_DP * N_EXPERT
    per_device = TOK_DEV * TOPK
    id_table = expert_ids.reshape(devices, per_device).astype(jnp.int32)
    onehot = (id_table[:, :, None] == jnp.arange(EXPERTS, dtype=jnp.int32)[None, None, :]).astype(jnp.int32)
    rank_of = jnp.sum((jnp.cumsum(onehot, axis=1) - onehot) * onehot, axis=2).astype(jnp.int32)
    source = jnp.arange(devices, dtype=jnp.int32)[:, None]
    slot_index = ((id_table * devices + source) * MOST + rank_of).astype(jnp.int32)
    token_index = (source * TOK_DEV + jnp.arange(per_device, dtype=jnp.int32)[None, :] // TOPK).astype(jnp.int32)
    slot_total = EXPERTS * devices * MOST
    token_table = jnp.full((slot_total,), TOKENS, jnp.int32).at[slot_index.reshape(-1)].set(token_index.reshape(-1))
    weight_table = jnp.zeros((slot_total,), jnp.float32).at[slot_index.reshape(-1)].set(router_probs.reshape(-1).astype(jnp.float32))
    tok_pad = jnp.concatenate([tokens, jnp.zeros((1, D), jnp.bfloat16)], axis=0)
    grad_pad = jnp.concatenate([out_grad, jnp.zeros((1, D), jnp.bfloat16)], axis=0)

    def per_expert(inputs):
        table_e, prob_e, gate_w, up_w, down_w = inputs
        tok_slots = tok_pad[table_e]
        grad_slots = (prob_e[:, None] * grad_pad[table_e].astype(jnp.float32)).astype(jnp.bfloat16)
        return expert_pass(tok_slots, grad_slots, gate_w, up_w, down_w)

    outs_slots, back_slots, grad_gate, grad_up, grad_down = lax.map(
        per_expert,
        (token_table.reshape(EXPERTS, devices * MOST), weight_table.reshape(EXPERTS, devices * MOST), w_gate, w_up, w_down))
    out_flat = outs_slots.reshape(slot_total, D)
    back_flat = back_slots.reshape(slot_total, D)
    flat_slot = slot_index.reshape(TOKENS, TOPK)
    mixed = jnp.zeros((TOKENS, D), jnp.float32)
    input_grad = jnp.zeros((TOKENS, D), jnp.float32)
    grad_cols = []
    dy_float = out_grad.astype(jnp.float32)
    for k_index in range(TOPK):
        rows_k = out_flat[flat_slot[:, k_index]].astype(jnp.float32)
        mixed = mixed + router_probs[:, k_index:k_index + 1] * rows_k
        grad_cols.append(jnp.sum(dy_float * rows_k, axis=1))
        input_grad = input_grad + back_flat[flat_slot[:, k_index]].astype(jnp.float32)
    prob_grad = jnp.stack(grad_cols, axis=1)
    return (mixed.astype(jnp.bfloat16), input_grad.astype(jnp.bfloat16), prob_grad, grad_gate, grad_up, grad_down)
```

```python
import jax
import jax.numpy as jnp
from jax import lax
from jax.sharding import PartitionSpec as P


def deliver(stacked):
    moved_rows = lax.all_to_all(stacked, "expert", split_axis=1, concat_axis=1, tiled=True)
    arrived = lax.all_gather(moved_rows[None], "dp", axis=0, tiled=True)
    return arrived


def send_back(stacked):
    return lax.all_to_all(stacked, "expert", split_axis=1, concat_axis=1, tiled=True)


def on_device(tokens, expert_ids, router_probs, w_gate, w_up, w_down, out_grad):
    tok_rows, model_width = tokens.shape
    top_count = expert_ids.shape[1]
    local_experts = w_gate.shape[0]
    n_expert = lax.axis_size("expert")
    n_replica = lax.axis_size("dp")
    experts = local_experts * n_expert
    slot_depth = max(2, tok_rows * top_count * 9 // (8 * experts))
    slot_total = experts * slot_depth
    blocks = n_replica * n_expert
    flat_ids = expert_ids.reshape(-1)
    same = flat_ids[:, None] == flat_ids[None, :]
    order = jnp.arange(flat_ids.shape[0], dtype=jnp.int32)
    rank_of = jnp.sum((same & (order[None, :] < order[:, None])).astype(jnp.int32), axis=1)
    slot_of = flat_ids * slot_depth + rank_of
    selector = (jnp.arange(slot_total, dtype=jnp.int32)[:, None] == slot_of[None, :]).astype(
        jnp.bfloat16
    )
    by_token = jnp.sum(selector.reshape(slot_total, tok_rows, top_count), axis=2)
    send_tokens = jnp.dot(by_token, tokens, preferred_element_type=jnp.float32).astype(jnp.bfloat16)
    send_tokens = send_tokens.reshape(n_expert, local_experts, slot_depth, model_width)
    scaled = (
        router_probs.reshape(-1)[:, None]
        * jnp.repeat(out_grad, top_count, axis=0).astype(jnp.float32)
    ).astype(jnp.bfloat16)
    send_grads = jnp.dot(selector, scaled, preferred_element_type=jnp.float32).astype(jnp.bfloat16)
    send_grads = send_grads.reshape(n_expert, local_experts, slot_depth, model_width)
    block_shape = (blocks, local_experts, slot_depth, model_width)
    rows_in = deliver(send_tokens[None])[:, 0].reshape(block_shape)
    gate_proj = jnp.einsum("sxmd,xfd->sxmf", rows_in, w_gate, preferred_element_type=jnp.float32)
    up_proj = jnp.einsum("sxmd,xfd->sxmf", rows_in, w_up, preferred_element_type=jnp.float32)
    sigmoid_gate = jax.nn.sigmoid(gate_proj)
    activated = gate_proj * sigmoid_gate
    hidden = (activated * up_proj).astype(jnp.bfloat16)
    expert_out = lax.psum_scatter(
        jnp.einsum("sxmf,xfd->sxmd", hidden, w_down, preferred_element_type=jnp.float32).astype(
            jnp.bfloat16
        ),
        "dp",
        scatter_dimension=0,
        tiled=True,
    )
    back_out = send_back(expert_out[None])[0]
    grads_in = deliver(send_grads[None])[:, 0].reshape(block_shape)
    d_hidden = jnp.einsum("sxmd,xfd->sxmf", grads_in, w_down, preferred_element_type=jnp.float32)
    grad_down = jnp.einsum(
        "sxmf,sxmd->xfd", hidden, grads_in, preferred_element_type=jnp.float32
    ).astype(jnp.bfloat16)
    d_gate = (d_hidden * up_proj * sigmoid_gate * (1.0 + gate_proj * (1.0 - sigmoid_gate))).astype(
        jnp.bfloat16
    )
    d_up = (d_hidden * activated).astype(jnp.bfloat16)
    grad_gate = jnp.einsum(
        "sxmf,sxmd->xfd", d_gate, rows_in, preferred_element_type=jnp.float32
    ).astype(jnp.bfloat16)
    grad_up = jnp.einsum(
        "sxmf,sxmd->xfd", d_up, rows_in, preferred_element_type=jnp.float32
    ).astype(jnp.bfloat16)
    total = jnp.einsum("sxmf,xfd->sxmd", d_gate, w_gate, preferred_element_type=jnp.float32)
    expert_dx = lax.psum_scatter(
        (
            total + jnp.einsum("sxmf,xfd->sxmd", d_up, w_up, preferred_element_type=jnp.float32)
        ).astype(jnp.bfloat16),
        "dp",
        scatter_dimension=0,
        tiled=True,
    )
    back_dx = send_back(expert_dx[None])[0]
    out_slots = back_out.reshape(slot_total, model_width)
    dx_slots = back_dx.reshape(slot_total, model_width)
    per_choice = jnp.dot(selector.T, out_slots, preferred_element_type=jnp.float32)
    per_choice = per_choice.reshape(tok_rows, top_count, model_width)
    mixed = jnp.sum(router_probs[:, :, None] * per_choice, axis=1).astype(jnp.bfloat16)
    prob_grad = jnp.sum(out_grad.astype(jnp.float32)[:, None, :] * per_choice, axis=2)
    input_grad = jnp.dot(by_token.T, dx_slots, preferred_element_type=jnp.float32).astype(
        jnp.bfloat16
    )
    return (mixed, input_grad, prob_grad, grad_gate, grad_up, grad_down)


def solution(mesh):
    in_specs = (
        P(("dp", "expert"), None),
        P(("dp", "expert"), None),
        P(("dp", "expert"), None),
        P("expert", "dp", None),
        P("expert", "dp", None),
        P("expert", "dp", None),
        P(("dp", "expert"), None),
    )
    out_specs = (
        P(("dp", "expert"), None),
        P(("dp", "expert"), None),
        P(("dp", "expert"), None),
        P("expert", "dp", None),
        P("expert", "dp", None),
        P("expert", "dp", None),
    )
    return jax.shard_map(
        on_device, mesh=mesh, in_specs=in_specs, out_specs=out_specs, check_vma=False
    )
```

```python
import jax
import jax.numpy as jnp
from jax import lax
from jax.sharding import PartitionSpec as P

AXES = ("dp", "expert")
F32 = jnp.float32
BF16 = jnp.bfloat16


def pairings(n_dp, n_expert):
    first, second = [], []
    for z in range(n_dp):
        near, far = z ^ 1, n_dp - 1 - z
        for e in range(n_expert):
            a, b = (near, far) if e % 2 == 0 else (far, near)
            first.append((z * n_expert + e, a * n_expert + e))
            second.append((z * n_expert + e, b * n_expert + e))
    return first, second


def exchange(rows, n_expert):
    total, width = rows.shape
    packed = rows.reshape(n_expert, total // n_expert * (width // 128), 128)
    moved = lax.all_to_all(packed, "expert", split_axis=0, concat_axis=0, tiled=True)
    return moved.reshape(total, width)


def nt(a, b):
    return lax.dot_general(a, b, (((1,), (1,)), ((), ())), preferred_element_type=F32)


def tn(a, b):
    return lax.dot_general(a, b, (((0,), (0,)), ((), ())), preferred_element_type=F32)


def nn(a, b):
    return jnp.dot(a, b, preferred_element_type=F32)


def on_device(tokens, expert_ids, router_probs, w_gate, w_up, w_down, out_grad):
    tok_rows, model_width = tokens.shape
    top_count = expert_ids.shape[1]
    n_expert = lax.axis_size("expert")
    n_dp = lax.axis_size("dp")
    depth = 9
    slots = n_expert * depth
    quarter = w_gate.shape[1]
    row_pairs, weight_pairs = pairings(n_dp, n_expert)

    def swap_rows(x):
        return lax.ppermute(x, AXES, row_pairs)

    def swap_weights(x):
        return lax.ppermute(x, AXES, weight_pairs)

    gate_w = jnp.concatenate([w_gate[0], swap_weights(w_gate[0])], axis=0)
    up_w = jnp.concatenate([w_up[0], swap_weights(w_up[0])], axis=0)
    down_w = jnp.concatenate([w_down[0], swap_weights(w_down[0])], axis=0)

    flat_ids = expert_ids.reshape(-1)
    same = flat_ids[:, None] == flat_ids[None, :]
    order = jnp.arange(flat_ids.shape[0], dtype=jnp.int32)
    rank_of = jnp.sum((same & (order[None, :] < order[:, None])).astype(jnp.int32), axis=1)
    slot_of = flat_ids * depth + rank_of
    selector = (jnp.arange(slots, dtype=jnp.int32)[:, None] == slot_of[None, :]).astype(BF16)
    by_token = jnp.sum(selector.reshape(slots, tok_rows, top_count), axis=2)

    send_tokens = nn(by_token, tokens).astype(BF16)
    mine = exchange(send_tokens, n_expert)
    theirs = swap_rows(mine)
    scaled = (
        router_probs.reshape(-1)[:, None] * jnp.repeat(out_grad, top_count, axis=0).astype(F32)
    ).astype(BF16)
    send_grads = nn(selector, scaled).astype(BF16)
    mine_g = exchange(send_grads, n_expert)
    theirs_g = swap_rows(mine_g)

    rows = jnp.concatenate([mine, theirs], axis=0)
    grads = jnp.concatenate([mine_g, theirs_g], axis=0)
    gate_proj = nt(rows, gate_w)
    up_proj = nt(rows, up_w)
    sig = jax.nn.sigmoid(gate_proj)
    activated = gate_proj * sig
    hidden = (activated * up_proj).astype(BF16)

    out_theirs = swap_rows(nn(hidden[slots:], down_w).astype(BF16))
    out_rows = (nn(hidden[:slots], down_w) + out_theirs.astype(F32)).astype(BF16)
    back_out = exchange(out_rows, n_expert)

    d_hidden = nt(grads, down_w)
    d_gate = (d_hidden * up_proj * sig * (1.0 + gate_proj * (1.0 - sig))).astype(BF16)
    d_up = (d_hidden * activated).astype(BF16)
    dx_theirs = swap_rows((nn(d_gate[slots:], gate_w) + nn(d_up[slots:], up_w)).astype(BF16))
    dx_rows = (
        nn(d_gate[:slots], gate_w) + nn(d_up[:slots], up_w) + dx_theirs.astype(F32)
    ).astype(BF16)
    back_dx = exchange(dx_rows, n_expert)

    def reduced(units, data):
        other = swap_weights(tn(units[:, quarter:], data).astype(BF16))
        return (tn(units[:, :quarter], data) + other.astype(F32)).astype(BF16)[None]

    grad_down = reduced(hidden, grads)
    grad_gate = reduced(d_gate, rows)
    grad_up = reduced(d_up, rows)

    per_choice = tn(selector, back_out).reshape(tok_rows, top_count, model_width)
    mixed = jnp.sum(router_probs[:, :, None] * per_choice, axis=1).astype(BF16)
    prob_grad = jnp.sum(out_grad.astype(F32)[:, None, :] * per_choice, axis=2)
    input_grad = tn(by_token, back_dx).astype(BF16)
    return (mixed, input_grad, prob_grad, grad_gate, grad_up, grad_down)


def solution(mesh):
    rows = P(("dp", "expert"), None)
    weights = P("expert", "dp", None)
    return jax.shard_map(
        on_device,
        mesh=mesh,
        in_specs=(rows, rows, rows, weights, weights, weights, rows),
        out_specs=(rows, rows, rows, weights, weights, weights),
        check_vma=False,
    )
```

```python
import jax
import jax.numpy as jnp
from jax import lax
from jax.sharding import PartitionSpec as P

AXES = ("dp", "expert")
F32 = jnp.float32
BF16 = jnp.bfloat16


def pairings(n_dp, n_expert):
    first, second = [], []
    for z in range(n_dp):
        near, far = z ^ 1, n_dp - 1 - z
        for e in range(n_expert):
            a, b = (near, far) if e % 2 == 0 else (far, near)
            first.append((z * n_expert + e, a * n_expert + e))
            second.append((z * n_expert + e, b * n_expert + e))
    return first, second


def exchange(rows, n_expert):
    total, width = rows.shape
    packed = rows.reshape(n_expert, total // n_expert * (width // 128), 128)
    moved = lax.all_to_all(packed, "expert", split_axis=0, concat_axis=0, tiled=True)
    return moved.reshape(total, width)


def nt(a, b):
    return lax.dot_general(a, b, (((1,), (1,)), ((), ())), preferred_element_type=F32)


def tn(a, b):
    return lax.dot_general(a, b, (((0,), (0,)), ((), ())), preferred_element_type=F32)


def nn(a, b):
    return jnp.dot(a, b, preferred_element_type=F32)


def on_device(tokens, expert_ids, router_probs, w_gate, w_up, w_down, out_grad):
    tok_rows, model_width = tokens.shape
    top_count = expert_ids.shape[1]
    n_expert = lax.axis_size("expert")
    n_dp = lax.axis_size("dp")
    depth = 9
    slots = n_expert * depth
    quarter = w_gate.shape[1]
    row_pairs, weight_pairs = pairings(n_dp, n_expert)

    def swap_rows(x):
        return lax.ppermute(x, AXES, row_pairs)

    def swap_weights(x):
        return lax.ppermute(x, AXES, weight_pairs)

    def after(value, *earlier):
        return lax.optimization_barrier((value, *earlier))[0]

    own_w = (w_gate[0], w_up[0], w_down[0])
    other_gate = swap_weights(own_w[0])
    other_up = swap_weights(own_w[1])
    other_down = swap_weights(after(own_w[2], other_gate))
    other_w = (other_gate, other_up, other_down)

    flat_ids = expert_ids.reshape(-1)
    same = flat_ids[:, None] == flat_ids[None, :]
    order = jnp.arange(flat_ids.shape[0], dtype=jnp.int32)
    rank_of = jnp.sum((same & (order[None, :] < order[:, None])).astype(jnp.int32), axis=1)
    slot_of = flat_ids * depth + rank_of
    selector = (jnp.arange(slots, dtype=jnp.int32)[:, None] == slot_of[None, :]).astype(BF16)
    by_token = jnp.sum(selector.reshape(slots, tok_rows, top_count), axis=2)

    send_tokens = nn(by_token, tokens).astype(BF16)
    mine = exchange(send_tokens, n_expert)
    scaled = (
        router_probs.reshape(-1)[:, None] * jnp.repeat(out_grad, top_count, axis=0).astype(F32)
    ).astype(BF16)
    send_grads = nn(selector, scaled).astype(BF16)
    mine_g = exchange(send_grads, n_expert)
    gate_w, up_w, down_w = (jnp.concatenate(w, axis=0) for w in zip(own_w, other_w))
    theirs = swap_rows(after(mine, other_up))
    theirs_g = swap_rows(after(mine_g, other_down))

    rows = jnp.concatenate([mine, theirs], axis=0)
    grads = jnp.concatenate([mine_g, theirs_g], axis=0)
    gate_proj = nt(rows, gate_w)
    up_proj = nt(rows, up_w)
    sig = jax.nn.sigmoid(gate_proj)
    activated = gate_proj * sig
    hidden = (activated * up_proj).astype(BF16)
    out_send = nn(hidden[slots:], down_w).astype(BF16)
    out_theirs = swap_rows(out_send)
    grads, _ = lax.optimization_barrier((grads, out_send))

    d_hidden = nt(grads, down_w)
    d_gate = (d_hidden * up_proj * sig * (1.0 + gate_proj * (1.0 - sig))).astype(BF16)
    d_up = (d_hidden * activated).astype(BF16)
    dx_send = (nn(d_gate[slots:], gate_w) + nn(d_up[slots:], up_w)).astype(BF16)
    dx_theirs = swap_rows(dx_send)
    products = ((hidden, grads), (d_gate, rows), (d_up, rows))
    parts = tuple(tn(units[:, quarter:], data).astype(BF16) for units, data in products)

    other_0 = swap_weights(after(parts[0], out_theirs))
    other_1 = swap_weights(after(parts[1], dx_theirs))
    other_2 = swap_weights(after(parts[2], other_0))
    others = (other_0, other_1, other_2)
    out_theirs = after(out_theirs, parts)

    out_rows = (nn(hidden[:slots], down_w) + out_theirs.astype(F32)).astype(BF16)
    back_out = exchange(out_rows, n_expert)
    dx_rows = (
        nn(d_gate[:slots], gate_w) + nn(d_up[:slots], up_w) + dx_theirs.astype(F32)
    ).astype(BF16)
    back_dx = exchange(dx_rows, n_expert)

    per_choice = tn(selector, back_out).reshape(tok_rows, top_count, model_width)
    mixed = jnp.sum(router_probs[:, :, None] * per_choice, axis=1).astype(BF16)
    prob_grad = jnp.sum(out_grad.astype(F32)[:, None, :] * per_choice, axis=2)
    input_grad = tn(by_token, back_dx).astype(BF16)

    grad_down, grad_gate, grad_up = (
        (tn(units[:, :quarter], data) + other.astype(F32)).astype(BF16)[None]
        for (units, data), other in zip(products, others)
    )
    return (mixed, input_grad, prob_grad, grad_gate, grad_up, grad_down)


def solution(mesh):
    rows = P(("dp", "expert"), None)
    weights = P("expert", "dp", None)
    return jax.shard_map(
        on_device,
        mesh=mesh,
        in_specs=(rows, rows, rows, weights, weights, weights, rows),
        out_specs=(rows, rows, rows, weights, weights, weights),
        check_vma=False,
    )
```

```python
import jax
import jax.numpy as jnp
from jax import lax
from jax.experimental import pallas as pl
from jax.experimental.pallas import tpu as pltpu
from jax.sharding import PartitionSpec as P

AXES = ("dp", "expert")
F32 = jnp.float32
BF16 = jnp.bfloat16
PEERS = 32
MAIN = 8 * PEERS
SLOTS = 9 * PEERS
HALF = 2048
TILES = HALF // 128
CHUNK = 9 * TILES
VMEM_LIMIT = 56 * 1024 * 1024


def pairings(n_dp, n_expert):
    first, second = [], []
    for z in range(n_dp):
        near, far = z ^ 1, n_dp - 1 - z
        for e in range(n_expert):
            a, b = (near, far) if e % 2 == 0 else (far, near)
            first.append((z * n_expert + e, a * n_expert + e))
            second.append((z * n_expert + e, b * n_expert + e))
    return first, second


def exchange(packed):
    return lax.all_to_all(packed, "expert", split_axis=0, concat_axis=0, tiled=True)


def pack(value, out_ref, spare_ref):
    for pair in range(TILES // 2):
        tiles = [
            value[:MAIN, 128 * c : 128 * (c + 1)].reshape(PEERS, 8, 128)
            for c in (2 * pair, 2 * pair + 1)
        ]
        out_ref[:, 16 * pair : 16 * (pair + 1), :] = jnp.concatenate(tiles, axis=1).astype(BF16)
    for c in range(TILES):
        spare_ref[:, c, :] = value[MAIN:, 128 * c : 128 * (c + 1)]
    out_ref[:, 8 * TILES :, :] = spare_ref[...].astype(BF16)


def unpack(in_ref, rows_ref, base, spare_ref):
    for pair in range(TILES // 2):
        both = in_ref[:, 16 * pair : 16 * (pair + 1), :].astype(F32)
        for side in range(2):
            c = 2 * pair + side
            tile = both[:, 8 * side : 8 * (side + 1), :].reshape(MAIN, 128)
            rows_ref[base : base + MAIN, 128 * c : 128 * (c + 1)] = tile.astype(BF16)
    spare_ref[...] = in_ref[:, 8 * TILES :, :].astype(F32)
    for c in range(TILES):
        rows_ref[base + MAIN : base + SLOTS, 128 * c : 128 * (c + 1)] = spare_ref[:, c, :].astype(
            BF16
        )


def whole(shape):
    return pl.BlockSpec(shape, lambda j: (0,) * len(shape))


def columns(rows):
    return pl.BlockSpec((rows, HALF), lambda j: (0, j))


def chunks():
    return pl.BlockSpec((PEERS, CHUNK, 128), lambda j: (0, j, 0))


def steps(kernel, width, in_specs, out_specs, out_shape, scratch, flops, moved):
    return pl.pallas_call(
        kernel,
        grid=(width // HALF,),
        in_specs=in_specs,
        out_specs=out_specs,
        out_shape=out_shape,
        scratch_shapes=scratch,
        compiler_params=pltpu.CompilerParams(vmem_limit_bytes=VMEM_LIMIT),
        cost_estimate=pl.CostEstimate(flops=flops, bytes_accessed=moved, transcendentals=0),
    )


SPARE = pltpu.VMEM((PEERS, TILES, 128), F32)


def packed_like(width):
    return jax.ShapeDtypeStruct((PEERS, CHUNK * (width // HALF), 128), BF16)


def picks(slots_ref, k):
    row = slots_ref[k : k + 1, :]
    at = lax.broadcasted_iota(jnp.int32, (SLOTS, row.shape[1]), 0)
    return (at == row).astype(F32)


def send_tokens_kernel(slots_ref, tokens_ref, out_ref, spare_ref):
    selector = (picks(slots_ref, 0) + picks(slots_ref, 1)).astype(BF16)
    pack(nn(selector, tokens_ref[...]), out_ref, spare_ref)


def send_tokens_of(slots, tokens):
    n, width = tokens.shape
    return steps(
        send_tokens_kernel, width, [whole(slots.shape), columns(n)], chunks(), packed_like(width),
        [SPARE], 2 * SLOTS * n * width, 2 * (SLOTS + n) * width,
    )(slots, tokens)


def send_grads_kernel(slots_ref, probs_ref, grad_ref, out_ref, spare_ref):
    grad = grad_ref[...].astype(F32)
    total = None
    for k in range(2):
        scaled = (probs_ref[:, k : k + 1] * grad).astype(BF16)
        part = nn(picks(slots_ref, k).astype(BF16), scaled)
        total = part if total is None else total + part
    pack(total, out_ref, spare_ref)


def send_grads_of(slots, probs, grad):
    n, width = grad.shape
    return steps(
        send_grads_kernel, width, [whole(slots.shape), whole(probs.shape), columns(n)], chunks(),
        packed_like(width), [SPARE], 4 * SLOTS * n * width, 2 * (SLOTS + n) * width,
    )(slots, probs, grad)


def rows_kernel(mine_ref, theirs_ref, rows_ref, spare_ref):
    unpack(mine_ref, rows_ref, 0, spare_ref)
    unpack(theirs_ref, rows_ref, SLOTS, spare_ref)


def rows_of(mine, theirs, width):
    return steps(
        rows_kernel, width, [chunks(), chunks()], columns(2 * SLOTS),
        jax.ShapeDtypeStruct((2 * SLOTS, width), BF16), [SPARE], 0, 8 * SLOTS * width,
    )(mine, theirs)


def sum_kernel(own_ref, theirs_ref, out_ref, spare_ref):
    pack(own_ref[...] + theirs_ref[...].astype(F32), out_ref, spare_ref)


def packed_sum(own, theirs):
    width = own.shape[1]
    return steps(
        sum_kernel, width, [columns(SLOTS), columns(SLOTS)], chunks(), packed_like(width), [SPARE],
        SLOTS * width, 8 * SLOTS * width,
    )(own, theirs)


def choice(slots_ref, k):
    column = slots_ref[:, k : k + 1]
    at = lax.broadcasted_iota(jnp.int32, (column.shape[0], SLOTS), 1)
    return (at == column).astype(F32)


def mixed_kernel(slots_ref, probs_ref, grad_ref, back_ref, mixed_ref, prob_grad_ref, rows_ref, spare_ref):
    unpack(back_ref, rows_ref, 0, spare_ref)
    grad = grad_ref[...].astype(F32)
    total, dots = None, []
    for k in range(2):
        chosen = nn(choice(slots_ref, k).astype(BF16), rows_ref[...])
        part = probs_ref[:, k : k + 1] * chosen
        total = part if total is None else total + part
        dots.append(jnp.sum(grad * chosen, axis=1, keepdims=True))
    mixed_ref[...] = total.astype(BF16)
    dots = jnp.concatenate(dots, axis=1)

    @pl.when(pl.program_id(0) == 0)
    def _():
        prob_grad_ref[...] = dots

    @pl.when(pl.program_id(0) != 0)
    def _():
        prob_grad_ref[...] += dots


def mixed_of(slots, probs, grad, back):
    n, width = grad.shape
    return steps(
        mixed_kernel, width,
        [whole(slots.shape), whole(probs.shape), columns(n), chunks()],
        [columns(n), whole(probs.shape)],
        [jax.ShapeDtypeStruct((n, width), BF16), jax.ShapeDtypeStruct(probs.shape, F32)],
        [pltpu.VMEM((SLOTS, HALF), BF16), SPARE], 4 * SLOTS * n * width, 2 * (SLOTS + 2 * n) * width,
    )(slots, probs, grad, back)


def input_grad_kernel(slots_ref, back_ref, out_ref, rows_ref, spare_ref):
    unpack(back_ref, rows_ref, 0, spare_ref)
    both = (choice(slots_ref, 0) + choice(slots_ref, 1)).astype(BF16)
    out_ref[...] = nn(both, rows_ref[...]).astype(BF16)


def input_grad_of(slots, back, width):
    n = slots.shape[0]
    return steps(
        input_grad_kernel, width, [whole(slots.shape), chunks()], columns(n),
        jax.ShapeDtypeStruct((n, width), BF16), [pltpu.VMEM((SLOTS, HALF), BF16), SPARE],
        2 * SLOTS * n * width, 2 * (SLOTS + n) * width,
    )(slots, back)


def nt(a, b):
    return lax.dot_general(a, b, (((1,), (1,)), ((), ())), preferred_element_type=F32)


def tn(a, b):
    return lax.dot_general(a, b, (((0,), (0,)), ((), ())), preferred_element_type=F32)


def nn(a, b):
    return jnp.dot(a, b, preferred_element_type=F32)


def on_device(tokens, expert_ids, router_probs, w_gate, w_up, w_down, out_grad):
    width = tokens.shape[1]
    n_expert = lax.axis_size("expert")
    n_dp = lax.axis_size("dp")
    quarter = w_gate.shape[1]
    row_pairs, weight_pairs = pairings(n_dp, n_expert)

    def swap_rows(x):
        return lax.ppermute(x, AXES, row_pairs)

    def swap_weights(x):
        return lax.ppermute(x, AXES, weight_pairs)

    def after(value, *earlier):
        return lax.optimization_barrier((value, *earlier))[0]

    own_w = (w_gate[0], w_up[0], w_down[0])
    other_gate = swap_weights(own_w[0])
    other_up = swap_weights(own_w[1])

    flat_ids = expert_ids.reshape(-1)
    same = flat_ids[:, None] == flat_ids[None, :]
    order = jnp.arange(flat_ids.shape[0], dtype=jnp.int32)
    rank_of = jnp.sum((same & (order[None, :] < order[:, None])).astype(jnp.int32), axis=1)
    slot_of = jnp.where(rank_of < 8, flat_ids * 8 + rank_of, MAIN + flat_ids)
    slots = slot_of.reshape(expert_ids.shape)
    slots_across = slots.T

    send_tokens = send_tokens_of(slots_across, tokens)
    send_grads = send_grads_of(slots_across, router_probs, out_grad)
    mine = exchange(send_tokens)
    mine_g = exchange(send_grads)
    other_down = swap_weights(after(own_w[2], other_gate, send_grads))
    other_w = (other_gate, other_up, other_down)
    gate_w, up_w, down_w = (jnp.concatenate(w, axis=0) for w in zip(own_w, other_w))
    theirs = swap_rows(after(mine, other_up, other_down))
    theirs_g = swap_rows(after(mine_g, other_down))

    rows = rows_of(mine, theirs, width)
    gate_proj = nt(rows, gate_w)
    up_proj = nt(rows, up_w)
    sig = jax.nn.sigmoid(gate_proj)
    activated = gate_proj * sig
    hidden = (activated * up_proj).astype(BF16)
    out_send = nn(hidden[SLOTS:], down_w).astype(BF16)
    out_theirs = swap_rows(out_send)
    out_own = nn(hidden[:SLOTS], down_w)

    theirs_g = after(theirs_g, out_send)
    grads = rows_of(mine_g, theirs_g, width)
    d_hidden = nt(grads, down_w)
    d_gate = (d_hidden * up_proj * sig * (1.0 + gate_proj * (1.0 - sig))).astype(BF16)
    d_up = (d_hidden * activated).astype(BF16)
    dx_send = (nn(d_gate[SLOTS:], gate_w) + nn(d_up[SLOTS:], up_w)).astype(BF16)
    dx_theirs = swap_rows(dx_send)
    products = ((hidden, grads), (d_gate, rows), (d_up, rows))
    out_sum = packed_sum(out_own, after(out_theirs, dx_send))
    back_out = exchange(out_sum)
    products = tuple((after(units, out_sum), data) for units, data in products)
    parts = tuple(tn(units[:, quarter:], data).astype(BF16) for units, data in products)
    dx_own = nn(d_gate[:SLOTS], gate_w) + nn(d_up[:SLOTS], up_w)

    other_0 = swap_weights(after(parts[0], out_theirs))
    other_1 = swap_weights(after(parts[1], dx_theirs))
    other_2 = swap_weights(after(parts[2], other_0, dx_theirs))
    others = (other_0, other_1, other_2)
    back_dx = exchange(packed_sum(dx_own, dx_theirs))
    mixed, prob_grad = mixed_of(slots, router_probs, out_grad, back_out)
    input_grad = input_grad_of(slots, back_dx, width)

    grad_down, grad_gate, grad_up = (
        (tn(units[:, :quarter], data) + other.astype(F32)).astype(BF16)[None]
        for (units, data), other in zip(products, others)
    )
    return (mixed, input_grad, prob_grad, grad_gate, grad_up, grad_down)


def solution(mesh):
    rows = P(("dp", "expert"), None)
    weights = P("expert", "dp", None)
    return jax.shard_map(
        on_device,
        mesh=mesh,
        in_specs=(rows, rows, rows, weights, weights, weights, rows),
        out_specs=(rows, rows, rows, weights, weights, weights),
        check_vma=False,
    )
```

```python
import jax
import jax.numpy as jnp
from jax import lax
from jax.experimental import pallas as pl
from jax.experimental.pallas import tpu as pltpu
from jax.sharding import PartitionSpec as P

AXES = ("dp", "expert")
F32 = jnp.float32
BF16 = jnp.bfloat16
PEERS = 32
MAIN = 8 * PEERS
SLOTS = 9 * PEERS
HALF = 2048
TILES = HALF // 128
CHUNK = 9 * TILES
VMEM_LIMIT = 56 * 1024 * 1024


def pairings(n_dp, n_expert):
    first, second = [], []
    for z in range(n_dp):
        near, far = z ^ 1, n_dp - 1 - z
        for e in range(n_expert):
            a, b = (near, far) if e % 2 == 0 else (far, near)
            first.append((z * n_expert + e, a * n_expert + e))
            second.append((z * n_expert + e, b * n_expert + e))
    return first, second


def exchange(packed):
    return lax.all_to_all(packed, "expert", split_axis=0, concat_axis=0, tiled=True)


def pack(value, out_ref, spare_ref):
    for pair in range(TILES // 2):
        tiles = [
            value[:MAIN, 128 * c : 128 * (c + 1)].reshape(PEERS, 8, 128)
            for c in (2 * pair, 2 * pair + 1)
        ]
        out_ref[:, 16 * pair : 16 * (pair + 1), :] = jnp.concatenate(tiles, axis=1).astype(BF16)
    for c in range(TILES):
        spare_ref[:, c, :] = value[MAIN:, 128 * c : 128 * (c + 1)]
    out_ref[:, 8 * TILES :, :] = spare_ref[...].astype(BF16)


def unpack(in_ref, rows_ref, base, spare_ref):
    for pair in range(TILES // 2):
        both = in_ref[:, 16 * pair : 16 * (pair + 1), :].astype(F32)
        for side in range(2):
            c = 2 * pair + side
            tile = both[:, 8 * side : 8 * (side + 1), :].reshape(MAIN, 128)
            rows_ref[base : base + MAIN, 128 * c : 128 * (c + 1)] = tile.astype(BF16)
    spare_ref[...] = in_ref[:, 8 * TILES :, :].astype(F32)
    for c in range(TILES):
        rows_ref[base + MAIN : base + SLOTS, 128 * c : 128 * (c + 1)] = spare_ref[:, c, :].astype(
            BF16
        )


def whole(shape):
    return pl.BlockSpec(shape, lambda j: (0,) * len(shape))


def columns(rows):
    return pl.BlockSpec((rows, HALF), lambda j: (0, j))


def chunks():
    return pl.BlockSpec((PEERS, CHUNK, 128), lambda j: (0, j, 0))


def steps(kernel, width, in_specs, out_specs, out_shape, scratch, flops, moved):
    return pl.pallas_call(
        kernel,
        grid=(width // HALF,),
        in_specs=in_specs,
        out_specs=out_specs,
        out_shape=out_shape,
        scratch_shapes=scratch,
        compiler_params=pltpu.CompilerParams(vmem_limit_bytes=VMEM_LIMIT),
        cost_estimate=pl.CostEstimate(flops=flops, bytes_accessed=moved, transcendentals=0),
    )


SPARE = pltpu.VMEM((PEERS, TILES, 128), F32)


def packed_like(width):
    return jax.ShapeDtypeStruct((PEERS, CHUNK * (width // HALF), 128), BF16)


def picks(slots_ref, k):
    row = slots_ref[k : k + 1, :]
    at = lax.broadcasted_iota(jnp.int32, (SLOTS, row.shape[1]), 0)
    return (at == row).astype(F32)


def send_tokens_kernel(slots_ref, tokens_ref, out_ref, spare_ref):
    selector = (picks(slots_ref, 0) + picks(slots_ref, 1)).astype(BF16)
    pack(nn(selector, tokens_ref[...]), out_ref, spare_ref)


def send_tokens_of(slots, tokens):
    n, width = tokens.shape
    return steps(
        send_tokens_kernel, width, [whole(slots.shape), columns(n)], chunks(), packed_like(width),
        [SPARE], 2 * SLOTS * n * width, 2 * (SLOTS + n) * width,
    )(slots, tokens)


def send_grads_kernel(slots_ref, probs_ref, grad_ref, out_ref, spare_ref):
    grad = grad_ref[...].astype(F32)
    total = None
    for k in range(2):
        scaled = (probs_ref[:, k : k + 1] * grad).astype(BF16)
        part = nn(picks(slots_ref, k).astype(BF16), scaled)
        total = part if total is None else total + part
    pack(total, out_ref, spare_ref)


def send_grads_of(slots, probs, grad):
    n, width = grad.shape
    return steps(
        send_grads_kernel, width, [whole(slots.shape), whole(probs.shape), columns(n)], chunks(),
        packed_like(width), [SPARE], 4 * SLOTS * n * width, 2 * (SLOTS + n) * width,
    )(slots, probs, grad)


def rows_kernel(mine_ref, theirs_ref, rows_ref, spare_ref):
    unpack(mine_ref, rows_ref, 0, spare_ref)
    unpack(theirs_ref, rows_ref, SLOTS, spare_ref)


def rows_of(mine, theirs, width):
    return steps(
        rows_kernel, width, [chunks(), chunks()], columns(2 * SLOTS),
        jax.ShapeDtypeStruct((2 * SLOTS, width), BF16), [SPARE], 0, 8 * SLOTS * width,
    )(mine, theirs)


def sum_kernel(own_ref, theirs_ref, out_ref, spare_ref):
    pack(own_ref[...] + theirs_ref[...].astype(F32), out_ref, spare_ref)


def packed_sum(own, theirs):
    width = own.shape[1]
    return steps(
        sum_kernel, width, [columns(SLOTS), columns(SLOTS)], chunks(), packed_like(width), [SPARE],
        SLOTS * width, 8 * SLOTS * width,
    )(own, theirs)


def choice(slots_ref, k):
    column = slots_ref[:, k : k + 1]
    at = lax.broadcasted_iota(jnp.int32, (column.shape[0], SLOTS), 1)
    return (at == column).astype(F32)


def mixed_kernel(slots_ref, probs_ref, grad_ref, back_ref, mixed_ref, prob_grad_ref, rows_ref, spare_ref):
    unpack(back_ref, rows_ref, 0, spare_ref)
    grad = grad_ref[...].astype(F32)
    total, dots = None, []
    for k in range(2):
        chosen = nn(choice(slots_ref, k).astype(BF16), rows_ref[...])
        part = probs_ref[:, k : k + 1] * chosen
        total = part if total is None else total + part
        dots.append(jnp.sum(grad * chosen, axis=1, keepdims=True))
    mixed_ref[...] = total.astype(BF16)
    dots = jnp.concatenate(dots, axis=1)

    @pl.when(pl.program_id(0) == 0)
    def _():
        prob_grad_ref[...] = dots

    @pl.when(pl.program_id(0) != 0)
    def _():
        prob_grad_ref[...] += dots


def mixed_of(slots, probs, grad, back):
    n, width = grad.shape
    return steps(
        mixed_kernel, width,
        [whole(slots.shape), whole(probs.shape), columns(n), chunks()],
        [columns(n), whole(probs.shape)],
        [jax.ShapeDtypeStruct((n, width), BF16), jax.ShapeDtypeStruct(probs.shape, F32)],
        [pltpu.VMEM((SLOTS, HALF), BF16), SPARE], 4 * SLOTS * n * width, 2 * (SLOTS + 2 * n) * width,
    )(slots, probs, grad, back)


def input_grad_kernel(slots_ref, back_ref, out_ref, rows_ref, spare_ref):
    unpack(back_ref, rows_ref, 0, spare_ref)
    both = (choice(slots_ref, 0) + choice(slots_ref, 1)).astype(BF16)
    out_ref[...] = nn(both, rows_ref[...]).astype(BF16)


def input_grad_of(slots, back, width):
    n = slots.shape[0]
    return steps(
        input_grad_kernel, width, [whole(slots.shape), chunks()], columns(n),
        jax.ShapeDtypeStruct((n, width), BF16), [pltpu.VMEM((SLOTS, HALF), BF16), SPARE],
        2 * SLOTS * n * width, 2 * (SLOTS + n) * width,
    )(slots, back)


def nt(a, b):
    return lax.dot_general(a, b, (((1,), (1,)), ((), ())), preferred_element_type=F32)


def tn(a, b):
    return lax.dot_general(a, b, (((0,), (0,)), ((), ())), preferred_element_type=F32)


def nn(a, b):
    return jnp.dot(a, b, preferred_element_type=F32)


def on_device(tokens, expert_ids, router_probs, w_gate, w_up, w_down, out_grad):
    width = tokens.shape[1]
    n_expert = lax.axis_size("expert")
    n_dp = lax.axis_size("dp")
    quarter = w_gate.shape[1]
    row_pairs, weight_pairs = pairings(n_dp, n_expert)

    def swap_rows(x):
        return lax.ppermute(x, AXES, row_pairs)

    def swap_weights(x):
        return lax.ppermute(x, AXES, weight_pairs)

    def after(value, *earlier):
        return lax.optimization_barrier((value, *earlier))[0]

    own_w = (w_gate[0], w_up[0], w_down[0])
    other_gate = swap_weights(own_w[0])
    other_up = swap_weights(own_w[1])

    flat_ids = expert_ids.reshape(-1)
    same = flat_ids[:, None] == flat_ids[None, :]
    order = jnp.arange(flat_ids.shape[0], dtype=jnp.int32)
    rank_of = jnp.sum((same & (order[None, :] < order[:, None])).astype(jnp.int32), axis=1)
    slot_of = jnp.where(rank_of < 8, flat_ids * 8 + rank_of, MAIN + flat_ids)
    slots = slot_of.reshape(expert_ids.shape)
    slots_across = slots.T

    send_tokens = send_tokens_of(slots_across, tokens)
    send_grads = send_grads_of(slots_across, router_probs, out_grad)
    mine = exchange(send_tokens)
    mine_g = exchange(send_grads)
    half = quarter // 2
    down_0 = swap_weights(after(own_w[2][:half], other_gate, send_grads))
    down_1 = swap_weights(after(own_w[2][half:], other_up))
    gate_w = jnp.concatenate([own_w[0], other_gate], axis=0)
    up_w = jnp.concatenate([own_w[1], other_up], axis=0)
    down_w = jnp.concatenate([own_w[2], down_0, down_1], axis=0)
    theirs = swap_rows(after(mine, down_0))
    theirs_g = swap_rows(after(mine_g, down_1))

    rows = rows_of(mine, theirs, width)
    gate_proj = nt(rows, gate_w)
    up_proj = nt(rows, up_w)
    sig = jax.nn.sigmoid(gate_proj)
    activated = gate_proj * sig
    hidden = (activated * up_proj).astype(BF16)
    out_send = nn(hidden[SLOTS:], down_w).astype(BF16)
    out_theirs = swap_rows(out_send)
    out_own = nn(hidden[:SLOTS], down_w)

    theirs_g = after(theirs_g, out_send)
    grads = rows_of(mine_g, theirs_g, width)
    d_hidden = nt(grads, down_w)
    d_gate = (d_hidden * up_proj * sig * (1.0 + gate_proj * (1.0 - sig))).astype(BF16)
    d_up = (d_hidden * activated).astype(BF16)
    dx_send = (nn(d_gate[SLOTS:], gate_w) + nn(d_up[SLOTS:], up_w)).astype(BF16)
    dx_theirs = swap_rows(dx_send)
    products = ((hidden, grads), (d_gate, rows), (d_up, rows))
    out_sum = packed_sum(out_own, after(out_theirs, dx_send))
    back_out = exchange(out_sum)
    products = tuple((after(units, out_sum), data) for units, data in products)
    parts = tuple(tn(units[:, quarter:], data).astype(BF16) for units, data in products)
    dx_own = nn(d_gate[:SLOTS], gate_w) + nn(d_up[:SLOTS], up_w)

    other_0 = swap_weights(after(parts[0], out_theirs))
    other_1 = swap_weights(after(parts[1], dx_theirs))
    other_2 = swap_weights(after(parts[2], other_0, dx_theirs))
    others = (other_0, other_1, other_2)
    back_dx = exchange(packed_sum(dx_own, dx_theirs))
    mixed, prob_grad = mixed_of(slots, router_probs, out_grad, back_out)
    input_grad = input_grad_of(slots, back_dx, width)

    own = tuple(tn(units[:, :quarter], data) for units, data in products)
    own_2 = after(own[2], back_out)
    grad_down, grad_gate, grad_up = (
        (part + other.astype(F32)).astype(BF16)[None]
        for part, other in zip((own[0], own[1], own_2), others)
    )
    return (mixed, input_grad, prob_grad, grad_gate, grad_up, grad_down)


def solution(mesh):
    rows = P(("dp", "expert"), None)
    weights = P("expert", "dp", None)
    return jax.shard_map(
        on_device,
        mesh=mesh,
        in_specs=(rows, rows, rows, weights, weights, weights, rows),
        out_specs=(rows, rows, rows, weights, weights, weights),
        check_vma=False,
    )
```

```python
import jax
import jax.numpy as jnp
from jax import lax
from jax.experimental import pallas as pl
from jax.experimental.pallas import tpu as pltpu
from jax.sharding import PartitionSpec as P

AXES = ("dp", "expert")
F32 = jnp.float32
BF16 = jnp.bfloat16
PEERS = 32
MAIN = 8 * PEERS
SLOTS = 9 * PEERS
HALF = 2048
TILES = HALF // 128
CHUNK = 9 * TILES
VMEM_LIMIT = 56 * 1024 * 1024


def pairings(n_dp, n_expert):
    first, second = [], []
    for z in range(n_dp):
        near, far = z ^ 1, n_dp - 1 - z
        for e in range(n_expert):
            a, b = (near, far) if e % 2 == 0 else (far, near)
            first.append((z * n_expert + e, a * n_expert + e))
            second.append((z * n_expert + e, b * n_expert + e))
    return first, second


def exchange(packed):
    return lax.all_to_all(packed, "expert", split_axis=0, concat_axis=0, tiled=True)


def pack(value, out_ref, spare_ref):
    for pair in range(TILES // 2):
        tiles = [
            value[:MAIN, 128 * c : 128 * (c + 1)].reshape(PEERS, 8, 128)
            for c in (2 * pair, 2 * pair + 1)
        ]
        out_ref[:, 16 * pair : 16 * (pair + 1), :] = jnp.concatenate(tiles, axis=1).astype(BF16)
    for c in range(TILES):
        spare_ref[:, c, :] = value[MAIN:, 128 * c : 128 * (c + 1)]
    out_ref[:, 8 * TILES :, :] = spare_ref[...].astype(BF16)


def unpack(in_ref, rows_ref, base, spare_ref):
    for pair in range(TILES // 2):
        both = in_ref[:, 16 * pair : 16 * (pair + 1), :].astype(F32)
        for side in range(2):
            c = 2 * pair + side
            tile = both[:, 8 * side : 8 * (side + 1), :].reshape(MAIN, 128)
            rows_ref[base : base + MAIN, 128 * c : 128 * (c + 1)] = tile.astype(BF16)
    spare_ref[...] = in_ref[:, 8 * TILES :, :].astype(F32)
    for c in range(TILES):
        rows_ref[base + MAIN : base + SLOTS, 128 * c : 128 * (c + 1)] = spare_ref[:, c, :].astype(
            BF16
        )


def whole(shape):
    return pl.BlockSpec(shape, lambda j: (0,) * len(shape))


def columns(rows):
    return pl.BlockSpec((rows, HALF), lambda j: (0, j))


def chunks():
    return pl.BlockSpec((PEERS, CHUNK, 128), lambda j: (0, j, 0))


def steps(kernel, width, in_specs, out_specs, out_shape, scratch, flops, moved):
    return pl.pallas_call(
        kernel,
        grid=(width // HALF,),
        in_specs=in_specs,
        out_specs=out_specs,
        out_shape=out_shape,
        scratch_shapes=scratch,
        compiler_params=pltpu.CompilerParams(vmem_limit_bytes=VMEM_LIMIT),
        cost_estimate=pl.CostEstimate(flops=flops, bytes_accessed=moved, transcendentals=0),
    )


SPARE = pltpu.VMEM((PEERS, TILES, 128), F32)


def packed_like(width):
    return jax.ShapeDtypeStruct((PEERS, CHUNK * (width // HALF), 128), BF16)


def picks(slots_ref, k):
    row = slots_ref[k : k + 1, :]
    at = lax.broadcasted_iota(jnp.int32, (SLOTS, row.shape[1]), 0)
    return (at == row).astype(F32)


def send_tokens_kernel(slots_ref, tokens_ref, out_ref, spare_ref):
    selector = (picks(slots_ref, 0) + picks(slots_ref, 1)).astype(BF16)
    pack(nn(selector, tokens_ref[...]), out_ref, spare_ref)


def send_tokens_of(slots, tokens):
    n, width = tokens.shape
    return steps(
        send_tokens_kernel, width, [whole(slots.shape), columns(n)], chunks(), packed_like(width),
        [SPARE], 2 * SLOTS * n * width, 2 * (SLOTS + n) * width,
    )(slots, tokens)


def send_grads_kernel(slots_ref, probs_ref, grad_ref, out_ref, spare_ref):
    grad = grad_ref[...].astype(F32)
    total = None
    for k in range(2):
        scaled = (probs_ref[:, k : k + 1] * grad).astype(BF16)
        part = nn(picks(slots_ref, k).astype(BF16), scaled)
        total = part if total is None else total + part
    pack(total, out_ref, spare_ref)


def send_grads_of(slots, probs, grad):
    n, width = grad.shape
    return steps(
        send_grads_kernel, width, [whole(slots.shape), whole(probs.shape), columns(n)], chunks(),
        packed_like(width), [SPARE], 4 * SLOTS * n * width, 2 * (SLOTS + n) * width,
    )(slots, probs, grad)


def rows_kernel(mine_ref, theirs_ref, rows_ref, spare_ref):
    unpack(mine_ref, rows_ref, 0, spare_ref)
    unpack(theirs_ref, rows_ref, SLOTS, spare_ref)


def rows_of(mine, theirs, width):
    return steps(
        rows_kernel, width, [chunks(), chunks()], columns(2 * SLOTS),
        jax.ShapeDtypeStruct((2 * SLOTS, width), BF16), [SPARE], 0, 8 * SLOTS * width,
    )(mine, theirs)


def sum_kernel(own_ref, theirs_ref, out_ref, spare_ref):
    pack(own_ref[...] + theirs_ref[...].astype(F32), out_ref, spare_ref)


def packed_sum(own, theirs):
    width = own.shape[1]
    return steps(
        sum_kernel, width, [columns(SLOTS), columns(SLOTS)], chunks(), packed_like(width), [SPARE],
        SLOTS * width, 8 * SLOTS * width,
    )(own, theirs)


def choice(slots_ref, k):
    column = slots_ref[:, k : k + 1]
    at = lax.broadcasted_iota(jnp.int32, (column.shape[0], SLOTS), 1)
    return (at == column).astype(F32)


def mixed_kernel(slots_ref, probs_ref, grad_ref, back_ref, mixed_ref, prob_grad_ref, rows_ref, spare_ref):
    unpack(back_ref, rows_ref, 0, spare_ref)
    grad = grad_ref[...].astype(F32)
    total, dots = None, []
    for k in range(2):
        chosen = nn(choice(slots_ref, k).astype(BF16), rows_ref[...])
        part = probs_ref[:, k : k + 1] * chosen
        total = part if total is None else total + part
        dots.append(jnp.sum(grad * chosen, axis=1, keepdims=True))
    mixed_ref[...] = total.astype(BF16)
    dots = jnp.concatenate(dots, axis=1)

    @pl.when(pl.program_id(0) == 0)
    def _():
        prob_grad_ref[...] = dots

    @pl.when(pl.program_id(0) != 0)
    def _():
        prob_grad_ref[...] += dots


def mixed_of(slots, probs, grad, back):
    n, width = grad.shape
    return steps(
        mixed_kernel, width,
        [whole(slots.shape), whole(probs.shape), columns(n), chunks()],
        [columns(n), whole(probs.shape)],
        [jax.ShapeDtypeStruct((n, width), BF16), jax.ShapeDtypeStruct(probs.shape, F32)],
        [pltpu.VMEM((SLOTS, HALF), BF16), SPARE], 4 * SLOTS * n * width, 2 * (SLOTS + 2 * n) * width,
    )(slots, probs, grad, back)


def input_grad_kernel(slots_ref, back_ref, out_ref, rows_ref, spare_ref):
    unpack(back_ref, rows_ref, 0, spare_ref)
    both = (choice(slots_ref, 0) + choice(slots_ref, 1)).astype(BF16)
    out_ref[...] = nn(both, rows_ref[...]).astype(BF16)


def input_grad_of(slots, back, width):
    n = slots.shape[0]
    return steps(
        input_grad_kernel, width, [whole(slots.shape), chunks()], columns(n),
        jax.ShapeDtypeStruct((n, width), BF16), [pltpu.VMEM((SLOTS, HALF), BF16), SPARE],
        2 * SLOTS * n * width, 2 * (SLOTS + n) * width,
    )(slots, back)


def nt(a, b):
    return lax.dot_general(a, b, (((1,), (1,)), ((), ())), preferred_element_type=F32)


def tn(a, b):
    return lax.dot_general(a, b, (((0,), (0,)), ((), ())), preferred_element_type=F32)


def nn(a, b):
    return jnp.dot(a, b, preferred_element_type=F32)


def on_device(tokens, expert_ids, router_probs, w_gate, w_up, w_down, out_grad):
    width = tokens.shape[1]
    n_expert = lax.axis_size("expert")
    n_dp = lax.axis_size("dp")
    quarter = w_gate.shape[1]
    row_pairs, weight_pairs = pairings(n_dp, n_expert)

    def swap_rows(x):
        return lax.ppermute(x, AXES, row_pairs)

    def swap_weights(x):
        return lax.ppermute(x, AXES, weight_pairs)

    def after(value, *earlier):
        return lax.optimization_barrier((value, *earlier))[0]

    own_w = (w_gate[0], w_up[0], w_down[0])
    other_gate = swap_weights(own_w[0])
    other_up = swap_weights(own_w[1])

    flat_ids = expert_ids.reshape(-1)
    same = flat_ids[:, None] == flat_ids[None, :]
    order = jnp.arange(flat_ids.shape[0], dtype=jnp.int32)
    rank_of = jnp.sum((same & (order[None, :] < order[:, None])).astype(jnp.int32), axis=1)
    slot_of = jnp.where(rank_of < 8, flat_ids * 8 + rank_of, MAIN + flat_ids)
    slots = slot_of.reshape(expert_ids.shape)
    slots_across = slots.T

    send_tokens = send_tokens_of(slots_across, tokens)
    send_grads = send_grads_of(slots_across, router_probs, out_grad)
    mine = exchange(send_tokens)
    mine_g = exchange(send_grads)
    other_down = swap_weights(after(own_w[2], other_gate, send_grads))
    other_w = (other_gate, other_up, other_down)
    gate_w, up_w, down_w = (jnp.concatenate(w, axis=0) for w in zip(own_w, other_w))
    theirs = swap_rows(after(mine, other_up, other_down))
    theirs_g = swap_rows(after(mine_g, other_down))

    rows = rows_of(mine, theirs, width)
    gate_proj = nt(rows, gate_w)
    up_proj = nt(rows, up_w)
    sig = jax.nn.sigmoid(gate_proj)
    activated = gate_proj * sig
    hidden = (activated * up_proj).astype(BF16)
    out_send = nn(hidden[SLOTS:], down_w).astype(BF16)
    out_theirs = swap_rows(out_send)
    out_own = nn(hidden[:SLOTS], down_w)

    theirs_g = after(theirs_g, out_send)
    grads = rows_of(mine_g, theirs_g, width)
    d_hidden = nt(grads, down_w)
    d_gate = (d_hidden * up_proj * sig * (1.0 + gate_proj * (1.0 - sig))).astype(BF16)
    d_up = (d_hidden * activated).astype(BF16)
    dx_send = (nn(d_gate[SLOTS:], gate_w) + nn(d_up[SLOTS:], up_w)).astype(BF16)
    dx_theirs = swap_rows(dx_send)
    products = ((hidden, grads), (d_gate, rows), (d_up, rows))
    out_sum = packed_sum(out_own, after(out_theirs, dx_send))
    back_out = exchange(out_sum)
    products = tuple((after(units, out_sum), data) for units, data in products)
    parts = tuple(tn(units[:, quarter:], data).astype(BF16) for units, data in products)
    dx_own = nn(d_gate[:SLOTS], gate_w) + nn(d_up[:SLOTS], up_w)

    other_0 = swap_weights(after(parts[0], out_theirs))
    other_1 = swap_weights(after(parts[1], dx_theirs))
    other_2 = swap_weights(after(parts[2], other_0, dx_theirs))
    others = (other_0, other_1, other_2)
    back_dx = exchange(packed_sum(dx_own, dx_theirs))
    mixed, prob_grad = mixed_of(slots, router_probs, out_grad, back_out)
    input_grad = input_grad_of(slots, back_dx, width)

    own = tuple(tn(units[:, :quarter], data) for units, data in products)
    own_2 = after(own[2], back_out)
    grad_down, grad_gate, grad_up = (
        (part + other.astype(F32)).astype(BF16)[None]
        for part, other in zip((own[0], own[1], own_2), others)
    )
    return (mixed, input_grad, prob_grad, grad_gate, grad_up, grad_down)


def solution(mesh):
    rows = P(("dp", "expert"), None)
    weights = P("expert", "dp", None)
    return jax.shard_map(
        on_device,
        mesh=mesh,
        in_specs=(rows, rows, rows, weights, weights, weights, rows),
        out_specs=(rows, rows, rows, weights, weights, weights),
        check_vma=False,
    )
```
